512 devices in a mesh: dp: 16 (over y, x), mp: 32 (over z, core).
Axes of the slice: x: 4, y: 4, z: 16, core: 2. Of those that a mesh axis runs over, the one named last changes fastest.
Arguments:
- act_cand: bfloat16 [1024, 4096], P('mp', 'dp'), may hold values from -6 to 6
- outgrad_cand: bfloat16 [1024, 16384], P('dp', 'mp'), may hold values from -6 to 6
- act_query: bfloat16 [512, 4096], P('mp', 'dp'), may hold values from -6 to 6
- outgrad_query: bfloat16 [512, 16384], P('dp', 'mp'), may hold values from -6 to 6
- loss_mask: int32 [16, 32], replicated, may hold values 0 or 1
- in_basis: bfloat16 [1024, 4096], P(None, 'dp'), may hold values from -0.1875 to 0.1875
- out_basis: bfloat16 [1024, 16384], P(None, 'mp'), may hold values from -0.1875 to 0.1875
- eigvals: float32 [4096, 16384], P('dp', 'mp'), may hold values from 0.05 to 5
Outputs:
- scores: float32 [16, 2], replicated
The draws below stay inside these ranges and needn't reach their ends.
All inputs are finite; a program needn't handle non-finite values.
Results may differ from the reference program's by a relative error of at most 0.0048.
Values may be sent and summed in bfloat16 or wider, within the bound.
A program may use at most 64 MiB of HBM per device.

```python
import math
import jax
import jax.numpy as jnp
from jax import lax

DW = 4096
FW = 16384
BLK = 1024
QUERIES = 16
QLEN = 32
CLEN = 512
CANDS = 2
QTOKENS = 512
CTOKENS = 1024


def set_ends(values, own_key, low, top_value):
    longest = values.shape.index(max(values.shape))
    spots = []
    for shift in (0, 1):
        where = [jax.random.randint(jax.random.fold_in(own_key, axis), (), 0, length) for axis, length in enumerate(values.shape)]
        where[longest] = (where[longest] + shift) % values.shape[longest]
        spots.append(tuple(where))
    return values.at[spots[0]].set(low).at[spots[1]].set(top_value)


def levels(own_key, shape, split, smallest, top_value):
    loudness, own = 1.0, jax.random.fold_in(own_key, 6)
    for axis_at, blocks in split:
        draws = jnp.exp(jax.random.uniform(jax.random.fold_in(own, axis_at), (blocks,), jnp.float32, smallest / len(split), top_value / len(split)))
        loudness = loudness * jnp.repeat(draws, shape[axis_at] // blocks).reshape([-1 if axis == axis_at else 1 for axis in range(len(shape))])
    return loudness


def normal_values(rng, extent, spread, reach, shards=(), kind=jnp.bfloat16):
    result = jax.random.normal(rng, extent, jnp.float32) * spread
    if len(shards) > 0:
        result = levels(rng, extent, shards, -0.22, 0.18) * result
    return jnp.clip(result, min=-reach, max=reach).astype(kind)


def setup_inputs(seed: int = 0) -> dict:
    streams_of = jax.random.split(jax.random.key(seed), 9)
    act_cand = normal_values(streams_of[0], (CTOKENS, DW), 1.0, 6.0, ((0, 32), (1, 16)))
    outgrad_cand = normal_values(streams_of[1], (CTOKENS, FW), 1.0, 6.0, ((0, 16), (1, 32)))
    act_query = normal_values(streams_of[2], (QTOKENS, DW), 1.0, 6.0, ((0, 32), (1, 16)))
    outgrad_query = normal_values(streams_of[3], (QTOKENS, FW), 1.0, 6.0, ((0, 16), (1, 32)))
    loss_mask = set_ends((jax.random.randint(streams_of[4], (QUERIES, QLEN), 0, 4) < 3).astype(jnp.int32), jax.random.fold_in(streams_of[4], 1), 0, 1)
    in_basis = normal_values(streams_of[5], (BLK, DW), BLK ** -0.5, 0.1875, ((1, 16),))
    out_basis = normal_values(streams_of[6], (BLK, FW), BLK ** -0.5, 0.1875, ((1, 32),))
    eigvals = jnp.clip(jnp.exp(math.log(5.0) - 4.6051702 * jax.random.uniform(streams_of[7], (DW, FW), jnp.float32) ** levels(streams_of[7], (DW, FW), ((0, 16), (1, 32)), -0.2, 0.2)), 0.05, 5.0)
    return dict(act_cand=act_cand, outgrad_cand=outgrad_cand, act_query=act_query, outgrad_query=outgrad_query, loss_mask=loss_mask, in_basis=in_basis, out_basis=out_basis, eigvals=eigvals)


DAMPING = 0.1

def rotate(acts, basis):
    tokens_here = acts.shape[0]
    nblocks = acts.shape[1] // BLK
    turned = jnp.einsum('tbk,kbj->tbj', acts.reshape(tokens_here, nblocks, BLK).astype(jnp.float32), basis.reshape(BLK, nblocks, BLK).astype(jnp.float32), precision=lax.Precision.HIGHEST)
    return turned.reshape(tokens_here, nblocks * BLK).astype(jnp.bfloat16)

def reference(act_cand, outgrad_cand, act_query, outgrad_query, loss_mask, in_basis, out_basis, eigvals):
    in_cand = rotate(act_cand, in_basis)
    in_query = rotate(act_query, in_basis)
    out_cand = rotate(outgrad_cand, out_basis)
    out_query = rotate(outgrad_query, out_basis)
    mask_rows = loss_mask.reshape(QUERIES * QLEN, 1).astype(jnp.bfloat16)
    masked = in_query * mask_rows
    total = jnp.zeros((QUERIES, CANDS), jnp.float32)
    for first in range(DW // BLK):
        rows_in_q = masked[:, first * BLK:(first + 1) * BLK].astype(jnp.float32).reshape(QUERIES, QLEN, BLK)
        rows_in_c = in_cand[:, first * BLK:(first + 1) * BLK].astype(jnp.float32).reshape(CANDS, CLEN, BLK)
        for second in range(FW // BLK):
            cols_q = out_query[:, second * BLK:(second + 1) * BLK].astype(jnp.float32).reshape(QUERIES, QLEN, BLK)
            cols_c = out_cand[:, second * BLK:(second + 1) * BLK].astype(jnp.float32).reshape(CANDS, CLEN, BLK)
            query_grad = jnp.einsum('qti,qtj->qij', rows_in_q, cols_q, precision=lax.Precision.HIGHEST)
            values = eigvals[first * BLK:(first + 1) * BLK, second * BLK:(second + 1) * BLK]
            precond = (query_grad / (values + DAMPING)).astype(jnp.bfloat16)
            precond = lax.optimization_barrier(precond).astype(jnp.float32)
            cand_grad = jnp.einsum('cti,ctj->cij', rows_in_c, cols_c, precision=lax.Precision.HIGHEST)
            total = total + jnp.einsum('qij,cij->qc', precond, cand_grad, precision=lax.Precision.HIGHEST)
    return total * (1.0 / math.sqrt(QLEN * CLEN * DW * FW))
```

```python
import math

import jax
import jax.numpy as jnp
from jax import lax
from jax.experimental import pallas as pl
from jax.experimental.pallas import tpu as pltpu
from jax.sharding import PartitionSpec as P

DW = 4096
FW = 16384
QUERIES = 16
QLEN = 32
CLEN = 512
CANDS = 2
DAMPING = 0.1
SCALE = 1.0 / math.sqrt(QLEN * CLEN * DW * FW)

NX = 4
NZ = 16
CT, QT = 32, 16
CO, QO = 64, 32
WI, WO = 256, 512
HALF = (CO + QO) // 2

MESH = pl.DeviceIdType.MESH


def kernel(
    act_c, out_c, act_q, out_q, mask, in_basis, out_basis, eig,
    scores,
    actw, outw, basis_i, basis_o, eigv, maskv, maskcol, recip, in_all, out_all, part1, part2,
    load_sem, a_send, a_recv, b_send, b_recv, c_send, c_recv, pair_send, d_send, d_recv,
    e_send, e_recv, f_send, f_recv,
):
    dp = lax.axis_index("dp")
    mp = lax.axis_index("mp")
    y, x = dp // NX, dp % NX
    z, core = mp // 2, mp % 2
    partner = mp + 1 - 2 * core

    def at_z(step):
        return ((z + step + NZ) % NZ) * 2 + core

    def at_x(step):
        return y * NX + (x + step) % NX

    def at_y(step):
        return ((y + step) % NX) * NX + x

    def copy(src, dst, send, recv, to_dp, to_mp):
        return pltpu.make_async_remote_copy(
            src_ref=src, dst_ref=dst, send_sem=send, recv_sem=recv,
            device_id=(to_dp, to_mp), device_id_type=MESH,
        )

    loads = [
        pltpu.make_async_copy(act_c, actw.at[x, pl.ds(0, CT)], load_sem.at[0]),
        pltpu.make_async_copy(act_q, actw.at[x, pl.ds(CT, QT)], load_sem.at[1]),
        pltpu.make_async_copy(out_c, outw.at[core, pl.ds(0, CO)], load_sem.at[2]),
        pltpu.make_async_copy(out_q, outw.at[core, pl.ds(CO, QO)], load_sem.at[3]),
        pltpu.make_async_copy(out_basis, basis_o, load_sem.at[4]),
        pltpu.make_async_copy(in_basis, basis_i, load_sem.at[5]),
        pltpu.make_async_copy(mask, maskv, load_sem.at[6]),
        pltpu.make_async_copy(eig, eigv, load_sem.at[7]),
    ]

    barrier = pltpu.get_barrier_semaphore()
    greet = [(dp, partner)]
    greet += [(at_x(step), mp) for step in (1, 2, 3)]
    greet += [(at_y(step), mp) for step in (1, 2, 3)]
    greet += [(dp, at_z(step)) for step in (1, -1, 2, -2, 5, -5, 8)]
    for peer in greet:
        pl.semaphore_signal(barrier, inc=1, device_id=peer, device_id_type=MESH)
    for load in loads:
        load.start()
    for load in loads[:4]:
        load.wait()
    pl.semaphore_wait(barrier, len(greet))

    sends = []
    for step in (2, 1, 3):
        sends.append(copy(actw.at[x], actw.at[x], a_send.at[step], a_recv.at[step], at_x(step), mp))
    sends.append(copy(outw.at[core], outw.at[core], b_send, b_recv, dp, partner))
    for each in sends:
        each.start()

    loads[6].wait()
    rows = lax.broadcasted_iota(jnp.int32, (QLEN, QLEN), 0)
    lanes = lax.broadcasted_iota(jnp.int32, (QLEN, QLEN), 1)
    for q in range(QUERIES):
        spread = jnp.broadcast_to(maskv[pl.ds(q, 1), :].astype(jnp.float32), (QLEN, QLEN))
        column = jnp.sum(jnp.where(rows == lanes, spread, 0.0), axis=1, keepdims=True)
        maskcol[pl.ds(q * QLEN, QLEN), :] = jnp.broadcast_to(column, (QLEN, 128))
    loads[7].wait()
    recip[...] = 1.0 / (eigv[...] + DAMPING)

    loads[4].wait()
    sends[3].wait_recv()
    turned = jnp.dot(outw[0], basis_o[pl.ds(0, WO), :], preferred_element_type=jnp.float32)
    turned += jnp.dot(outw[1], basis_o[pl.ds(WO, WO), :], preferred_element_type=jnp.float32)
    out_all[dp] = turned.astype(jnp.bfloat16)

    def d_copy(half, slot, step, along_x, sem):
        rows = pl.ds(half * HALF, HALF)
        to_dp = at_x(step) if along_x else at_y(step)
        piece = out_all.at[slot, rows]
        return copy(piece, piece, d_send.at[sem], d_recv.at[half, slot], to_dp, mp)

    sem = 0
    for second in (False, True):
        for step in (2, 1, 3):
            for half in (0, 1):
                each = d_copy(half, dp, step, (half == 0) != second, sem)
                each.start()
                sends.append(each)
                sem += 1

    loads[5].wait()
    for each in sends[:3]:
        each.wait_recv()
    turned = jnp.dot(actw[0], basis_i[pl.ds(0, WI), :], preferred_element_type=jnp.float32)
    for piece in range(1, NX):
        turned += jnp.dot(
            actw[piece], basis_i[pl.ds(piece * WI, WI), :], preferred_element_type=jnp.float32
        )
    in_all[mp] = turned.astype(jnp.bfloat16)

    def c_copy(slot, step, sem):
        return copy(
            in_all.at[slot], in_all.at[slot], c_send.at[sem], c_recv.at[slot], dp, at_z(step)
        )

    def pair_copy(slot):
        return copy(
            in_all.at[slot], in_all.at[slot], pair_send.at[slot // 2], c_recv.at[slot], dp, partner
        )

    sem_c = 0
    for step in (8, 5, -5, 2, -2, 1, -1):
        each = c_copy(mp, step, sem_c)
        each.start()
        sends.append(each)
        sem_c += 1
    pair_copy(mp).start()

    for step in (1, 3, 2):
        for half in (0, 1):
            slot = at_x(step) if half == 0 else at_y(step)
            d_copy(half, slot, step, half == 0, 0).wait_recv()
            for onward in (2, 1, 3):
                each = d_copy(half, slot, onward, half == 1, sem)
                each.start()
                sends.append(each)
                sem += 1

    def arrive(step):
        slot = at_z(step)
        c_copy(slot, 1, 0).wait_recv()
        return slot

    for step in (1, -1, 2, -2):
        pair_copy(arrive(step)).start()
    for step in (5, -5):
        slot = arrive(step)
        for onward in (2, -2, 1, -1):
            each = c_copy(slot, onward, sem_c)
            each.start()
            sends.append(each)
            sem_c += 1
        pair_copy(slot).start()
    for step in (8, 4, -4, 6, -6, 3, -3, 7, -7):
        pair_copy(arrive(step)).start()

    for up in (1, 2, 3):
        for over in (1, 2, 3):
            slot = ((y + up) % NX) * NX + (x + over) % NX
            for half in (0, 1):
                d_copy(half, slot, 1, True, 0).wait_recv()
    for step in (1, 2, 3):
        d_copy(1, at_x(step), 1, True, 0).wait_recv()
        d_copy(0, at_y(step), 1, True, 0).wait_recv()

    def from_pair(step, carry):
        pair_copy(step * 2 + 1 - core).wait_recv()
        return carry

    lax.fori_loop(0, NZ, from_pair, 0)

    tokens = QUERIES * QLEN
    in_q = in_all[:, pl.ds(CT, QT), :].reshape(tokens, WI)
    folded = []
    for cand in range(CANDS):
        in_cand = in_all[pl.ds(cand * 16, 16), pl.ds(0, CT), :].reshape(CLEN, WI)
        out_cand = out_all[pl.ds(cand * 8, 8), pl.ds(0, CO), :].reshape(CLEN, WO)
        grad = lax.dot_general(
            in_cand, out_cand, (((0,), (0,)), ((), ())), preferred_element_type=jnp.float32
        )
        weight = (grad * recip[...]).astype(jnp.bfloat16)
        applied = jnp.dot(in_q, weight, preferred_element_type=jnp.float32)
        out_query = out_all[:, pl.ds(CO, QO), :].reshape(tokens, WO)
        product = applied * out_query.astype(jnp.float32)
        narrow = product[:, 0:128]
        for part in range(1, WO // 128):
            narrow += product[:, part * 128 : part * 128 + 128]
        narrow = narrow * maskcol[...]
        folded.append(jnp.sum(narrow.reshape(QUERIES, QLEN, 128), axis=1))
    column = jnp.sum(jnp.concatenate(folded, axis=0), axis=1, keepdims=True)
    count = QUERIES * CANDS
    rows = lax.broadcasted_iota(jnp.int32, (count, 128), 0)
    lanes = lax.broadcasted_iota(jnp.int32, (count, 128), 1)
    line = jnp.sum(
        jnp.where(rows == lanes, jnp.broadcast_to(column, (count, 128)), 0.0), axis=0, keepdims=True
    )

    flat = dp * 2 + core
    part1[flat] = line

    def e_copy(step):
        peer = (flat + step) % 32
        return copy(
            part1.at[flat], part1.at[flat], e_send.at[step], e_recv.at[step],
            peer // 2, z * 2 + peer % 2,
        )

    def e_start(step, carry):
        e_copy(step).start()
        return carry

    def e_wait(step, carry):
        e_copy(step).wait_recv()
        return carry

    lax.fori_loop(1, 32, e_start, 0)
    lax.fori_loop(1, 32, e_wait, 0)
    part2[z] = jnp.sum(part1[...], axis=0)

    def f_copy(step):
        return copy(
            part2.at[z], part2.at[z], f_send.at[step], f_recv.at[step], dp, at_z(step)
        )

    def f_start(step, carry):
        f_copy(step).start()
        return carry

    def f_wait(step, carry):
        f_copy(step).wait_recv()
        return carry

    lax.fori_loop(1, NZ, f_start, 0)
    lax.fori_loop(1, NZ, f_wait, 0)
    total = jnp.sum(part2[...], axis=0) * SCALE
    rows = lax.broadcasted_iota(jnp.int32, (QUERIES, 128), 0)
    lanes = lax.broadcasted_iota(jnp.int32, (QUERIES, 128), 1)
    spread = jnp.broadcast_to(total, (QUERIES, 128))
    for cand in range(CANDS):
        scores[:, pl.ds(cand, 1)] = jnp.sum(
            jnp.where(lanes == rows + cand * QUERIES, spread, 0.0), axis=1, keepdims=True
        )

    for each in sends:
        each.wait_send()

    def pair_sent(step, carry):
        pair_copy(step * 2 + core).wait_send()
        return carry

    lax.fori_loop(0, NZ, pair_sent, 0)

    def e_sent(step, carry):
        e_copy(step).wait_send()
        return carry

    lax.fori_loop(1, 32, e_sent, 0)

    def f_sent(step, carry):
        f_copy(step).wait_send()
        return carry

    lax.fori_loop(1, NZ, f_sent, 0)


def local(*args):
    dma = pltpu.SemaphoreType.DMA
    return pl.pallas_call(
        kernel,
        name="scores",
        out_shape=jax.ShapeDtypeStruct((QUERIES, CANDS), jnp.float32),
        in_specs=[pl.BlockSpec(memory_space=pl.ANY)] * 8,
        out_specs=pl.BlockSpec(memory_space=pltpu.VMEM),
        scratch_shapes=[
            pltpu.VMEM((NX, CT + QT, WI), jnp.bfloat16),
            pltpu.VMEM((2, CO + QO, WO), jnp.bfloat16),
            pltpu.VMEM((NX * WI, WI), jnp.bfloat16),
            pltpu.VMEM((2 * WO, WO), jnp.bfloat16),
            pltpu.VMEM((WI, WO), jnp.float32),
            pltpu.VMEM((QUERIES, QLEN), jnp.int32),
            pltpu.VMEM((QUERIES * QLEN, 128), jnp.float32),
            pltpu.VMEM((WI, WO), jnp.float32),
            pltpu.VMEM((2 * NZ, CT + QT, WI), jnp.bfloat16),
            pltpu.VMEM((NX * NX, CO + QO, WO), jnp.bfloat16),
            pltpu.VMEM((32, 1, 128), jnp.float32),
            pltpu.VMEM((NZ, 1, 128), jnp.float32),
            dma((8,)),
            dma((NX,)),
            dma((NX,)),
            dma,
            dma,
            dma((15,)),
            dma((2 * NZ,)),
            dma((NZ,)),
            dma((30,)),
            dma((2, NX * NX)),
            dma((32,)),
            dma((32,)),
            dma((NZ,)),
            dma((NZ,)),
        ],
        compiler_params=pltpu.CompilerParams(
            collective_id=0, has_side_effects=True, vmem_limit_bytes=48 << 20
        ),
    )(*args)


def solution(mesh):
    return jax.shard_map(
        local,
        mesh=mesh,
        in_specs=(
            P("mp", "dp"),
            P("dp", "mp"),
            P("mp", "dp"),
            P("dp", "mp"),
            P(),
            P(None, "dp"),
            P(None, "mp"),
            P("dp", "mp"),
        ),
        out_specs=P(),
        check_vma=False,
    )
```

```python
import math

import jax
import jax.numpy as jnp
from jax import lax
from jax.experimental import pallas as pl
from jax.experimental.pallas import tpu as pltpu
from jax.sharding import PartitionSpec as P

DW = 4096
FW = 16384
QUERIES = 16
QLEN = 32
CLEN = 512
CANDS = 2
DAMPING = 0.1
FAR, NEAR = (5, -5), (2, -2, 1, -1)
ONWARD = (2, 1, -1, -2)
LAST = 3
GREET = (2, -2, 1, -1)
VOUCH = (2, 1)
REST = (4, -4, 6, -6, 3, -3, 7, -7, 8)
SCALE = 1.0 / math.sqrt(QLEN * CLEN * DW * FW)

NX = 4
NZ = 16
CT, QT = 32, 16
CO, QO = 64, 32
WI, WO = 256, 512
HALF = (CO + QO) // 2

MESH = pl.DeviceIdType.MESH


def kernel(
    act_c, out_c, act_q, out_q, mask, in_basis, out_basis, eig,
    scores,
    actw, outw, basis_i, basis_o, eigv, maskv, maskcol, recip, in_all, out_all, part1, part2,
    load_sem, a_send, a_recv, b_send, b_recv, c_send, c_recv, pair_send, d_send, d_recv,
    e_send, e_recv, f_send, f_recv, known,
):
    dp = lax.axis_index("dp")
    mp = lax.axis_index("mp")
    y, x = dp // NX, dp % NX
    z, core = mp // 2, mp % 2
    partner = mp + 1 - 2 * core

    def at_z(step):
        return ((z + step + NZ) % NZ) * 2 + core

    def at_x(step):
        return y * NX + (x + step) % NX

    def at_y(step):
        return ((y + step) % NX) * NX + x

    def copy(src, dst, send, recv, to_dp, to_mp):
        return pltpu.make_async_remote_copy(
            src_ref=src, dst_ref=dst, send_sem=send, recv_sem=recv,
            device_id=(to_dp, to_mp), device_id_type=MESH,
        )

    loads = [
        pltpu.make_async_copy(act_c, actw.at[x, pl.ds(0, CT)], load_sem.at[0]),
        pltpu.make_async_copy(act_q, actw.at[x, pl.ds(CT, QT)], load_sem.at[1]),
        pltpu.make_async_copy(out_c, outw.at[core, pl.ds(0, CO)], load_sem.at[2]),
        pltpu.make_async_copy(out_q, outw.at[core, pl.ds(CO, QO)], load_sem.at[3]),
        pltpu.make_async_copy(out_basis, basis_o, load_sem.at[4]),
        pltpu.make_async_copy(in_basis, basis_i, load_sem.at[5]),
        pltpu.make_async_copy(mask, maskv, load_sem.at[6]),
        pltpu.make_async_copy(eig, eigv, load_sem.at[7]),
    ]

    barrier = pltpu.get_barrier_semaphore()
    greet = [(dp, at_z(step)) for step in GREET]
    greet += [(at_x(step), mp) for step in (2, 1, 3)]
    greet += [(at_y(step), mp) for step in (2, 1, 3)]
    greet += [(dp, partner)]
    for peer in greet:
        pl.semaphore_signal(barrier, inc=1, device_id=peer, device_id_type=MESH)
    for load in loads:
        load.start()
    pl.semaphore_wait(barrier, len(greet))

    def vouch(level, reach):
        for step in (reach, -reach):
            pl.semaphore_signal(
                known.at[level], inc=1, device_id=(dp, at_z(step)), device_id_type=MESH
            )

    sends = []
    a_copies = []
    for step in (2, 1, 3):
        for part, (src, first, count) in enumerate(((act_c, 0, CT), (act_q, CT, QT))):
            a_copies.append(copy(
                src, actw.at[x, pl.ds(first, count)], a_send.at[step, part], a_recv.at[step, part],
                at_x(step), mp,
            ))
    b_copies = []
    for part, (src, first, count) in enumerate(((out_c, 0, CO), (out_q, CO, QO))):
        b_copies.append(copy(
            src, outw.at[core, pl.ds(first, count)], b_send.at[part], b_recv.at[part], dp, partner
        ))
    sends += a_copies + b_copies
    for each in sends:
        each.start()
    vouch(0, VOUCH[0])

    for load in loads[2:5]:
        load.wait()
    for each in b_copies:
        each.wait_recv()
    turned = jnp.dot(outw[0], basis_o[pl.ds(0, WO), :], preferred_element_type=jnp.float32)
    turned += jnp.dot(outw[1], basis_o[pl.ds(WO, WO), :], preferred_element_type=jnp.float32)
    out_all[dp] = turned.astype(jnp.bfloat16)

    def d_copy(half, slot, step, along_x, sem):
        rows = pl.ds(half * HALF, HALF)
        to_dp = at_x(step) if along_x else at_y(step)
        piece = out_all.at[slot, rows]
        return copy(piece, piece, d_send.at[sem], d_recv.at[half, slot], to_dp, mp)

    sem_d = 0

    def d_own(second):
        nonlocal sem_d
        for step in (2, 1, 3):
            for half in (0, 1):
                each = d_copy(half, dp, step, (half == 0) != second, sem_d)
                each.start()
                sends.append(each)
                sem_d += 1

    d_own(False)
    for level, reach in enumerate(VOUCH[1:]):
        pl.semaphore_wait(known.at[level], 2)
        vouch(level + 1, reach)

    for load in (loads[0], loads[1], loads[5]):
        load.wait()
    for each in a_copies:
        each.wait_recv()
    turned = jnp.dot(actw[0], basis_i[pl.ds(0, WI), :], preferred_element_type=jnp.float32)
    for piece in range(1, NX):
        turned += jnp.dot(
            actw[piece], basis_i[pl.ds(piece * WI, WI), :], preferred_element_type=jnp.float32
        )
    in_all[mp] = turned.astype(jnp.bfloat16)

    def c_copy(slot, step, sem):
        return copy(
            in_all.at[slot], in_all.at[slot], c_send.at[sem], c_recv.at[slot], dp, at_z(step)
        )

    def pair_copy(slot):
        return copy(
            in_all.at[slot], in_all.at[slot], pair_send.at[slot // 2], c_recv.at[slot], dp, partner
        )

    sem_c = 0

    def c_out(slot, steps):
        nonlocal sem_c
        for step in steps:
            each = c_copy(slot, step, sem_c)
            each.start()
            sends.append(each)
            sem_c += 1

    def arrive(step):
        slot = at_z(step)
        c_copy(slot, 1, 0).wait_recv()
        return slot

    pl.semaphore_wait(known.at[len(VOUCH) - 1], 2)
    c_out(mp, FAR + NEAR)
    pair_copy(mp).start()
    d_own(True)

    loads[6].wait()
    rows = lax.broadcasted_iota(jnp.int32, (QLEN, QLEN), 0)
    lanes = lax.broadcasted_iota(jnp.int32, (QLEN, QLEN), 1)
    for q in range(QUERIES):
        spread = jnp.broadcast_to(maskv[pl.ds(q, 1), :].astype(jnp.float32), (QLEN, QLEN))
        column = jnp.sum(jnp.where(rows == lanes, spread, 0.0), axis=1, keepdims=True)
        maskcol[pl.ds(q * QLEN, QLEN), :] = jnp.broadcast_to(column, (QLEN, 128))
    loads[7].wait()
    recip[...] = 1.0 / (eigv[...] + DAMPING)

    for step in (1, 3, 2):
        for half in (0, 1):
            slot = at_x(step) if half == 0 else at_y(step)
            d_copy(half, slot, step, half == 0, 0).wait_recv()
            for onward in (2, 1, 3):
                each = d_copy(half, slot, onward, half == 1, sem_d)
                each.start()
                sends.append(each)
                sem_d += 1

    for step in FAR:
        arrive(step)
    c_out(at_z((2 * core - 1) * FAR[0]), (LAST - 2 * LAST * core,))
    for onward in ONWARD:
        for step in FAR:
            c_out(at_z(step), (-onward if step > 0 else onward,))
    for step in FAR:
        pair_copy(at_z(step)).start()
    for step in NEAR + REST:
        pair_copy(arrive(step)).start()

    for up in (1, 2, 3):
        for over in (1, 2, 3):
            slot = ((y + up) % NX) * NX + (x + over) % NX
            for half in (0, 1):
                d_copy(half, slot, 1, True, 0).wait_recv()
    for step in (1, 2, 3):
        d_copy(1, at_x(step), 1, True, 0).wait_recv()
        d_copy(0, at_y(step), 1, True, 0).wait_recv()

    def from_pair(step, carry):
        pair_copy(step * 2 + 1 - core).wait_recv()
        return carry

    lax.fori_loop(0, NZ, from_pair, 0)

    tokens = QUERIES * QLEN
    in_q = in_all[:, pl.ds(CT, QT), :].reshape(tokens, WI)
    folded = []
    for cand in range(CANDS):
        in_cand = in_all[pl.ds(cand * 16, 16), pl.ds(0, CT), :].reshape(CLEN, WI)
        out_cand = out_all[pl.ds(cand * 8, 8), pl.ds(0, CO), :].reshape(CLEN, WO)
        grad = lax.dot_general(
            in_cand, out_cand, (((0,), (0,)), ((), ())), preferred_element_type=jnp.float32
        )
        weight = (grad * recip[...]).astype(jnp.bfloat16)
        applied = jnp.dot(in_q, weight, preferred_element_type=jnp.float32)
        out_query = out_all[:, pl.ds(CO, QO), :].reshape(tokens, WO)
        product = applied * out_query.astype(jnp.float32)
        narrow = product[:, 0:128]
        for part in range(1, WO // 128):
            narrow += product[:, part * 128 : part * 128 + 128]
        narrow = narrow * maskcol[...]
        folded.append(jnp.sum(narrow.reshape(QUERIES, QLEN, 128), axis=1))
    column = jnp.sum(jnp.concatenate(folded, axis=0), axis=1, keepdims=True)
    count = QUERIES * CANDS
    rows = lax.broadcasted_iota(jnp.int32, (count, 128), 0)
    lanes = lax.broadcasted_iota(jnp.int32, (count, 128), 1)
    line = jnp.sum(
        jnp.where(rows == lanes, jnp.broadcast_to(column, (count, 128)), 0.0), axis=0, keepdims=True
    )

    flat = dp * 2 + core
    part1[flat] = line
    plane = [(up, over, other) for up in range(NX) for over in range(NX) for other in range(2)]
    plane.sort(key=lambda o: (-min(o[0], NX - o[0]) - min(o[1], NX - o[1]), -o[2]))
    plane.remove((0, 0, 0))
    e_copies = []
    for index, (up, over, other) in enumerate(plane):
        to_dp = ((y + up) % NX) * NX + (x + over) % NX
        to_core = (core + other) % 2
        e_copies.append(copy(
            part1.at[flat], part1.at[flat], e_send.at[index], e_recv.at[index],
            to_dp, z * 2 + to_core,
        ))
    for each in e_copies:
        each.start()
    for each in reversed(e_copies):
        each.wait_recv()
    part2[z] = jnp.sum(part1[...], axis=0)

    f_copies = []
    for step in (8, 7, -7, 6, -6, 5, -5, 4, -4, 3, -3, 2, -2, 1, -1):
        f_copies.append(copy(
            part2.at[z], part2.at[z], f_send.at[step % NZ], f_recv.at[step % NZ], dp, at_z(step)
        ))
    for each in f_copies:
        each.start()
    for each in sends + e_copies:
        each.wait_send()

    def pair_sent(step, carry):
        pair_copy(step * 2 + core).wait_send()
        return carry

    lax.fori_loop(0, NZ, pair_sent, 0)
    for each in f_copies:
        each.wait_send()
    for each in reversed(f_copies):
        each.wait_recv()
    total = jnp.sum(part2[...], axis=0) * SCALE
    rows = lax.broadcasted_iota(jnp.int32, (QUERIES, 128), 0)
    lanes = lax.broadcasted_iota(jnp.int32, (QUERIES, 128), 1)
    spread = jnp.broadcast_to(total, (QUERIES, 128))
    for cand in range(CANDS):
        scores[:, pl.ds(cand, 1)] = jnp.sum(
            jnp.where(lanes == rows + cand * QUERIES, spread, 0.0), axis=1, keepdims=True
        )


def local(*args):
    dma = pltpu.SemaphoreType.DMA
    return pl.pallas_call(
        kernel,
        name="scores",
        out_shape=jax.ShapeDtypeStruct((QUERIES, CANDS), jnp.float32),
        in_specs=[pl.BlockSpec(memory_space=pl.ANY)] * 8,
        out_specs=pl.BlockSpec(memory_space=pltpu.VMEM),
        scratch_shapes=[
            pltpu.VMEM((NX, CT + QT, WI), jnp.bfloat16),
            pltpu.VMEM((2, CO + QO, WO), jnp.bfloat16),
            pltpu.VMEM((NX * WI, WI), jnp.bfloat16),
            pltpu.VMEM((2 * WO, WO), jnp.bfloat16),
            pltpu.VMEM((WI, WO), jnp.float32),
            pltpu.VMEM((QUERIES, QLEN), jnp.int32),
            pltpu.VMEM((QUERIES * QLEN, 128), jnp.float32),
            pltpu.VMEM((WI, WO), jnp.float32),
            pltpu.VMEM((2 * NZ, CT + QT, WI), jnp.bfloat16),
            pltpu.VMEM((NX * NX, CO + QO, WO), jnp.bfloat16),
            pltpu.VMEM((32, 1, 128), jnp.float32),
            pltpu.VMEM((NZ, 1, 128), jnp.float32),
            dma((8,)),
            dma((NX, 2)),
            dma((NX, 2)),
            dma((2,)),
            dma((2,)),
            dma((15,)),
            dma((2 * NZ,)),
            dma((NZ,)),
            dma((30,)),
            dma((2, NX * NX)),
            dma((32,)),
            dma((32,)),
            dma((NZ,)),
            dma((NZ,)),
            pltpu.SemaphoreType.REGULAR((3,)),
        ],
        compiler_params=pltpu.CompilerParams(
            collective_id=0, has_side_effects=True, vmem_limit_bytes=60 << 20
        ),
    )(*args)


def solution(mesh):
    return jax.shard_map(
        local,
        mesh=mesh,
        in_specs=(
            P("mp", "dp"),
            P("dp", "mp"),
            P("mp", "dp"),
            P("dp", "mp"),
            P(),
            P(None, "dp"),
            P(None, "mp"),
            P("dp", "mp"),
        ),
        out_specs=P(),
        check_vma=False,
    )
```

```python
import functools
import math

import jax
import jax.numpy as jnp
from jax import lax
from jax.experimental import pallas as pl
from jax.experimental.pallas import tpu as pltpu
from jax.sharding import PartitionSpec as P

DW = 4096
FW = 16384
QUERIES = 16
QLEN = 32
CLEN = 512
CANDS = 2
DAMPING = 0.1
FAR, NEAR = (5, -5), (2, -2, 1, -1)
ONWARD = (2, 1, -1, -2)
LAST = 3
GREET = (2, -2, 1, -1)
VOUCH = (2, 1)
REST = (4, -4, 6, -6, 3, -3, 7, -7, 8)
SCALE = 1.0 / math.sqrt(QLEN * CLEN * DW * FW)

NX = 4
NZ = 16
CT, QT = 32, 16
CO, QO = 64, 32
WI, WO = 256, 512
HALF = (CO + QO) // 2

MESH = pl.DeviceIdType.MESH


def kernel(
    act_c, out_c, act_q, out_q, mask, in_basis, out_basis, eig,
    scores,
    actw, outw, basis_i, basis_o, eigv, maskv, maskcol, recip, in_all, out_all, part1, part2,
    load_sem, a_send, a_recv, b_send, b_recv, c_send, c_recv, pair_send, d_send, d_recv,
    e_send, e_recv, f_send, f_recv, pair_recv, d_rest, known,
):
    dp = lax.axis_index("dp")
    mp = lax.axis_index("mp")
    y, x = lax.div(dp, NX), lax.rem(dp, NX)
    z, core = lax.div(mp, 2), lax.rem(mp, 2)
    partner = mp + 1 - 2 * core

    def at_z(step):
        return lax.rem(z + step + NZ, NZ) * 2 + core

    @functools.cache
    def in_plane(up, over):
        return lax.rem(y + up, NX) * NX + lax.rem(x + over, NX)

    def at_x(step):
        return in_plane(0, step)

    def at_y(step):
        return in_plane(step, 0)

    def copy(src, dst, send, recv, to_dp, to_mp):
        return pltpu.make_async_remote_copy(
            src_ref=src, dst_ref=dst, send_sem=send, recv_sem=recv,
            device_id=(to_dp, to_mp), device_id_type=MESH,
        )

    loads = [
        pltpu.make_async_copy(act_c, actw.at[x, pl.ds(0, CT)], load_sem.at[0]),
        pltpu.make_async_copy(act_q, actw.at[x, pl.ds(CT, QT)], load_sem.at[1]),
        pltpu.make_async_copy(out_c, outw.at[core, pl.ds(0, CO)], load_sem.at[2]),
        pltpu.make_async_copy(out_q, outw.at[core, pl.ds(CO, QO)], load_sem.at[3]),
        pltpu.make_async_copy(out_basis, basis_o, load_sem.at[4]),
        pltpu.make_async_copy(in_basis, basis_i, load_sem.at[5]),
        pltpu.make_async_copy(mask, maskv, load_sem.at[6]),
        pltpu.make_async_copy(eig, eigv, load_sem.at[7]),
    ]

    barrier = pltpu.get_barrier_semaphore()
    greet = [(dp, at_z(step)) for step in GREET]
    greet += [(at_x(step), mp) for step in (2, 1, 3)]
    greet += [(at_y(step), mp) for step in (2, 1, 3)]
    greet += [(dp, partner)]
    for peer in greet:
        pl.semaphore_signal(barrier, inc=1, device_id=peer, device_id_type=MESH)
    for load in loads:
        load.start()
    pl.semaphore_wait(barrier, len(greet))

    def vouch(level, reach):
        for step in (reach, -reach):
            pl.semaphore_signal(
                known.at[level], inc=1, device_id=(dp, at_z(step)), device_id_type=MESH
            )

    sends = []
    a_copies = []
    for step in (2, 1, 3):
        for part, (src, first, count) in enumerate(((act_c, 0, CT), (act_q, CT, QT))):
            a_copies.append(copy(
                src, actw.at[x, pl.ds(first, count)], a_send.at[step, part], a_recv.at[step, part],
                at_x(step), mp,
            ))
    b_copies = []
    for part, (src, first, count) in enumerate(((out_c, 0, CO), (out_q, CO, QO))):
        b_copies.append(copy(
            src, outw.at[core, pl.ds(first, count)], b_send.at[part], b_recv.at[part], dp, partner
        ))
    sends += a_copies + b_copies
    for each in sends:
        each.start()
    vouch(0, VOUCH[0])

    for load in loads[2:5]:
        load.wait()
    for each in b_copies:
        each.wait_recv()
    turned = jnp.dot(outw[0], basis_o[pl.ds(0, WO), :], preferred_element_type=jnp.float32)
    turned += jnp.dot(outw[1], basis_o[pl.ds(WO, WO), :], preferred_element_type=jnp.float32)
    out_all[dp] = turned.astype(jnp.bfloat16)

    def d_copy(half, slot, step, first):
        to_dp = at_x(step) if (half == 0) == first else at_y(step)
        part = out_all.at[slot, pl.ds(half * HALF, HALF)]
        return copy(part, part, d_send, d_recv.at[half, step] if first else d_rest, to_dp, mp)

    def d_own(first):
        for step in (2, 1, 3):
            for half in (0, 1):
                d_copy(half, dp, step, first).start()

    d_own(True)
    for level, reach in enumerate(VOUCH[1:]):
        pl.semaphore_wait(known.at[level], 2)
        vouch(level + 1, reach)

    loads[6].wait()
    rows = lax.broadcasted_iota(jnp.int32, (QLEN, QLEN), 0)
    lanes = lax.broadcasted_iota(jnp.int32, (QLEN, QLEN), 1)
    for q in range(QUERIES):
        spread = jnp.broadcast_to(maskv[pl.ds(q, 1), :].astype(jnp.float32), (QLEN, QLEN))
        column = jnp.sum(jnp.where(rows == lanes, spread, 0.0), axis=1, keepdims=True)
        maskcol[pl.ds(q * QLEN, QLEN), :] = jnp.broadcast_to(column, (QLEN, 128))
    loads[7].wait()
    recip[...] = 1.0 / (eigv[...] + DAMPING)

    for load in (loads[0], loads[1], loads[5]):
        load.wait()
    for each in a_copies:
        each.wait_recv()
    turned = jnp.dot(actw[0], basis_i[pl.ds(0, WI), :], preferred_element_type=jnp.float32)
    for piece in range(1, NX):
        turned += jnp.dot(
            actw[piece], basis_i[pl.ds(piece * WI, WI), :], preferred_element_type=jnp.float32
        )
    in_all[mp] = turned.astype(jnp.bfloat16)

    def c_copy(slot, step):
        return copy(
            in_all.at[slot], in_all.at[slot], c_send, c_recv.at[slot], dp, at_z(step)
        )

    def pair_copy(slot):
        return copy(
            in_all.at[slot], in_all.at[slot], pair_send, pair_recv, dp, partner
        )

    def c_out(slot, steps):
        for step in steps:
            c_copy(slot, step).start()

    def arrive(step):
        slot = at_z(step)
        c_copy(slot, 1).wait_recv()
        return slot

    pl.semaphore_wait(known.at[len(VOUCH) - 1], 2)
    c_out(mp, FAR + NEAR)
    pair_copy(mp).start()
    d_own(False)

    def d_onward(steps):
        for step in steps:
            for half in (0, 1):
                slot = at_x(step) if half == 0 else at_y(step)
                d_copy(half, slot, NX - step, True).wait_recv()
                for onward in (2, 1, 3):
                    d_copy(half, slot, onward, False).start()

    def c_onward(step):
        slot = arrive(step)
        for onward in ONWARD:
            c_out(slot, (-onward if step > 0 else onward,))

    def c_last():
        c_out(at_z((2 * core - 1) * FAR[0]), (LAST - 2 * LAST * core,))

    def c_pair(steps):
        for step in steps:
            pair_copy(arrive(step)).start()

    d_onward((1, 3, 2))
    c_onward(FAR[0])
    c_onward(FAR[1])
    c_last()
    for step in FAR:
        pair_copy(at_z(step)).start()
    c_pair(NEAR + REST)

    rest = out_all.at[pl.ds(0, 12)]
    pltpu.make_async_copy(rest, rest, d_rest).wait()
    half_line = in_all.at[pl.ds(0, NZ)]
    pltpu.make_async_copy(half_line, half_line, pair_recv).wait()

    tokens = QUERIES * QLEN
    in_q = in_all[:, pl.ds(CT, QT), :].reshape(tokens, WI)
    folded = []
    for cand in range(CANDS):
        in_cand = in_all[pl.ds(cand * 16, 16), pl.ds(0, CT), :].reshape(CLEN, WI)
        out_cand = out_all[pl.ds(cand * 8, 8), pl.ds(0, CO), :].reshape(CLEN, WO)
        grad = lax.dot_general(
            in_cand, out_cand, (((0,), (0,)), ((), ())), preferred_element_type=jnp.float32
        )
        weight = (grad * recip[...]).astype(jnp.bfloat16)
        applied = jnp.dot(in_q, weight, preferred_element_type=jnp.float32)
        out_query = out_all[:, pl.ds(CO, QO), :].reshape(tokens, WO)
        product = applied * out_query.astype(jnp.float32)
        narrow = product[:, 0:128]
        for part in range(1, WO // 128):
            narrow += product[:, part * 128 : part * 128 + 128]
        narrow = narrow * maskcol[...]
        folded.append(jnp.sum(narrow.reshape(QUERIES, QLEN, 128), axis=1))
    column = jnp.sum(jnp.concatenate(folded, axis=0), axis=1, keepdims=True)
    count = QUERIES * CANDS
    rows = lax.broadcasted_iota(jnp.int32, (count, 128), 0)
    lanes = lax.broadcasted_iota(jnp.int32, (count, 128), 1)
    line = jnp.sum(
        jnp.where(rows == lanes, jnp.broadcast_to(column, (count, 128)), 0.0), axis=0, keepdims=True
    )

    flat = dp * 2 + core
    part1[flat] = line
    plane = [(up, over, other) for up in range(NX) for over in range(NX) for other in range(2)]
    plane.sort(key=lambda o: (-min(o[0], NX - o[0]) - min(o[1], NX - o[1]), -o[2]))
    plane.remove((0, 0, 0))
    e_copies = []
    for index, (up, over, other) in enumerate(plane):
        e_copies.append(copy(
            part1.at[flat], part1.at[flat], e_send, e_recv,
            in_plane(up, over), partner if other else mp,
        ))
    for each in e_copies:
        each.start()
    others = part1.at[pl.ds(0, len(e_copies))]
    pltpu.make_async_copy(others, others, e_recv).wait()
    part2[z] = jnp.sum(part1[...], axis=0)

    f_copies = []
    for step in (8, 7, -7, 6, -6, 5, -5, 4, -4, 3, -3, 2, -2, 1, -1):
        f_copies.append(copy(
            part2.at[z], part2.at[z], f_send, f_recv, dp, at_z(step)
        ))
    for each in f_copies:
        each.start()
    for each in sends:
        each.wait_send()
    pltpu.make_async_copy(others, others, e_send).wait()
    gone = in_all.at[pl.ds(0, NZ - 1)]
    pltpu.make_async_copy(gone, gone, c_send).wait()
    gone = out_all.at[pl.ds(0, 15)]
    pltpu.make_async_copy(gone, gone, d_send).wait()

    pltpu.make_async_copy(half_line, half_line, pair_send).wait()
    others = part2.at[pl.ds(0, len(f_copies))]
    pltpu.make_async_copy(others, others, f_send).wait()
    pltpu.make_async_copy(others, others, f_recv).wait()
    total = jnp.sum(part2[...], axis=0) * SCALE
    rows = lax.broadcasted_iota(jnp.int32, (QUERIES, 128), 0)
    lanes = lax.broadcasted_iota(jnp.int32, (QUERIES, 128), 1)
    spread = jnp.broadcast_to(total, (QUERIES, 128))
    for cand in range(CANDS):
        scores[:, pl.ds(cand, 1)] = jnp.sum(
            jnp.where(lanes == rows + cand * QUERIES, spread, 0.0), axis=1, keepdims=True
        )


def local(*args):
    dma = pltpu.SemaphoreType.DMA
    return pl.pallas_call(
        kernel,
        name="scores",
        out_shape=jax.ShapeDtypeStruct((QUERIES, CANDS), jnp.float32),
        in_specs=[pl.BlockSpec(memory_space=pl.ANY)] * 8,
        out_specs=pl.BlockSpec(memory_space=pltpu.VMEM),
        scratch_shapes=[
            pltpu.VMEM((NX, CT + QT, WI), jnp.bfloat16),
            pltpu.VMEM((2, CO + QO, WO), jnp.bfloat16),
            pltpu.VMEM((NX * WI, WI), jnp.bfloat16),
            pltpu.VMEM((2 * WO, WO), jnp.bfloat16),
            pltpu.VMEM((WI, WO), jnp.float32),
            pltpu.VMEM((QUERIES, QLEN), jnp.int32),
            pltpu.VMEM((QUERIES * QLEN, 128), jnp.float32),
            pltpu.VMEM((WI, WO), jnp.float32),
            pltpu.VMEM((2 * NZ, CT + QT, WI), jnp.bfloat16),
            pltpu.VMEM((NX * NX, CO + QO, WO), jnp.bfloat16),
            pltpu.VMEM((32, 1, 128), jnp.float32),
            pltpu.VMEM((NZ, 1, 128), jnp.float32),
            dma((8,)),
            dma((NX, 2)),
            dma((NX, 2)),
            dma((2,)),
            dma((2,)),
            dma,
            dma((2 * NZ,)),
            dma,
            dma,
            dma((2, NX)),
            dma,
            dma,
            dma,
            dma,
            dma,
            dma,
            pltpu.SemaphoreType.REGULAR((3,)),
        ],
        compiler_params=pltpu.CompilerParams(
            collective_id=0, has_side_effects=True, vmem_limit_bytes=60 << 20
        ),
    )(*args)


def solution(mesh):
    return jax.shard_map(
        local,
        mesh=mesh,
        in_specs=(
            P("mp", "dp"),
            P("dp", "mp"),
            P("mp", "dp"),
            P("dp", "mp"),
            P(),
            P(None, "dp"),
            P(None, "mp"),
            P("dp", "mp"),
        ),
        out_specs=P(),
        check_vma=False,
    )
```

```python
import functools
import math

import jax
import jax.numpy as jnp
from jax import lax
from jax.experimental import pallas as pl
from jax.experimental.pallas import tpu as pltpu
from jax.sharding import PartitionSpec as P

DW = 4096
FW = 16384
QUERIES = 16
QLEN = 32
CLEN = 512
CANDS = 2
DAMPING = 0.1
FAR, NEAR = (5, -5), (2, -2, 1, -1)
ONWARD = (2, 1, -1, -2)
LAST = 3
GREET = (2, -2, 1, -1)
VOUCH = (2, 1)
REST = (4, -4, 6, -6, 3, -3, 7, -7, 8)
SCALE = 1.0 / math.sqrt(QLEN * CLEN * DW * FW)

NX = 4
NZ = 16
CT, QT = 32, 16
CO, QO = 64, 32
WI, WO = 256, 512
HALF = (CO + QO) // 2

MESH = pl.DeviceIdType.MESH


def kernel(
    act_c, out_c, act_q, out_q, mask, in_basis, out_basis, eig,
    scores,
    actw, outw, basis_i, basis_o, eigv, maskv, maskcol, recip, in_all, out_all, part1, part2,
    load_sem, a_send, a_recv, b_send, b_recv, c_send, c_recv, pair_send, d_send, d_recv,
    e_send, e_recv, f_send, f_recv, pair_recv, d_rest, known,
):
    dp = lax.axis_index("dp")
    mp = lax.axis_index("mp")
    y, x = lax.div(dp, NX), lax.rem(dp, NX)
    z, core = lax.div(mp, 2), lax.rem(mp, 2)
    partner = mp + 1 - 2 * core

    def at_z(step):
        return lax.rem(z + step + NZ, NZ) * 2 + core

    @functools.cache
    def in_plane(up, over):
        return lax.rem(y + up, NX) * NX + lax.rem(x + over, NX)

    def at_x(step):
        return in_plane(0, step)

    def at_y(step):
        return in_plane(step, 0)

    def copy(src, dst, send, recv, to_dp, to_mp):
        return pltpu.make_async_remote_copy(
            src_ref=src, dst_ref=dst, send_sem=send, recv_sem=recv,
            device_id=(to_dp, to_mp), device_id_type=MESH,
        )

    loads = [
        pltpu.make_async_copy(act_c, actw.at[x, pl.ds(0, CT)], load_sem.at[0]),
        pltpu.make_async_copy(act_q, actw.at[x, pl.ds(CT, QT)], load_sem.at[1]),
        pltpu.make_async_copy(out_c, outw.at[core, pl.ds(0, CO)], load_sem.at[2]),
        pltpu.make_async_copy(out_q, outw.at[core, pl.ds(CO, QO)], load_sem.at[3]),
        pltpu.make_async_copy(out_basis, basis_o, load_sem.at[4]),
        pltpu.make_async_copy(in_basis, basis_i, load_sem.at[5]),
        pltpu.make_async_copy(mask, maskv, load_sem.at[6]),
        pltpu.make_async_copy(eig, eigv, load_sem.at[7]),
    ]

    barrier = pltpu.get_barrier_semaphore()
    greet = [(dp, at_z(step)) for step in GREET]
    greet += [(at_x(step), mp) for step in (2, 1, 3)]
    greet += [(at_y(step), mp) for step in (2, 1, 3)]
    greet += [(dp, partner)]
    for peer in greet:
        pl.semaphore_signal(barrier, inc=1, device_id=peer, device_id_type=MESH)
    for load in loads[2:5]:
        load.start()
    pl.semaphore_wait(barrier, len(greet))

    def vouch(level, reach):
        for step in (reach, -reach):
            pl.semaphore_signal(
                known.at[level], inc=1, device_id=(dp, at_z(step)), device_id_type=MESH
            )

    vouch(0, VOUCH[0])

    sends = []
    a_copies = []
    for step in (2, 1, 3):
        for part, (src, first, count) in enumerate(((act_c, 0, CT), (act_q, CT, QT))):
            a_copies.append(copy(
                src, actw.at[x, pl.ds(first, count)], a_send.at[step, part], a_recv.at[step, part],
                at_x(step), mp,
            ))
    b_copies = []
    for part, (src, first, count) in enumerate(((out_c, 0, CO), (out_q, CO, QO))):
        b_copies.append(copy(
            src, outw.at[core, pl.ds(first, count)], b_send.at[part], b_recv.at[part], dp, partner
        ))
    sends += a_copies + b_copies
    for each in sends:
        each.start()
    for load in loads[:2] + loads[5:]:
        load.start()

    for load in loads[2:5]:
        load.wait()
    for each in b_copies:
        each.wait_recv()
    turned = jnp.dot(outw[0], basis_o[pl.ds(0, WO), :], preferred_element_type=jnp.float32)
    turned += jnp.dot(outw[1], basis_o[pl.ds(WO, WO), :], preferred_element_type=jnp.float32)
    out_all[dp] = turned.astype(jnp.bfloat16)

    def d_copy(half, slot, step, first):
        to_dp = at_x(step) if (half == 0) == first else at_y(step)
        part = out_all.at[slot, pl.ds(half * HALF, HALF)]
        return copy(part, part, d_send, d_recv.at[half, step] if first else d_rest, to_dp, mp)

    def d_own(first):
        for step in (2, 1, 3):
            for half in (0, 1):
                d_copy(half, dp, step, first).start()

    d_own(True)
    for level, reach in enumerate(VOUCH[1:]):
        pl.semaphore_wait(known.at[level], 2)
        vouch(level + 1, reach)

    loads[6].wait()
    rows = lax.broadcasted_iota(jnp.int32, (QLEN, QLEN), 0)
    lanes = lax.broadcasted_iota(jnp.int32, (QLEN, QLEN), 1)
    for q in range(QUERIES):
        spread = jnp.broadcast_to(maskv[pl.ds(q, 1), :].astype(jnp.float32), (QLEN, QLEN))
        column = jnp.sum(jnp.where(rows == lanes, spread, 0.0), axis=1, keepdims=True)
        maskcol[pl.ds(q * QLEN, QLEN), :] = jnp.broadcast_to(column, (QLEN, 128))
    loads[7].wait()
    recip[...] = 1.0 / (eigv[...] + DAMPING)

    for load in (loads[0], loads[1], loads[5]):
        load.wait()
    for each in a_copies:
        each.wait_recv()
    turned = jnp.dot(actw[0], basis_i[pl.ds(0, WI), :], preferred_element_type=jnp.float32)
    for piece in range(1, NX):
        turned += jnp.dot(
            actw[piece], basis_i[pl.ds(piece * WI, WI), :], preferred_element_type=jnp.float32
        )
    in_all[mp] = turned.astype(jnp.bfloat16)

    def c_copy(slot, step):
        return copy(
            in_all.at[slot], in_all.at[slot], c_send, c_recv.at[slot], dp, at_z(step)
        )

    def pair_copy(slot):
        return copy(
            in_all.at[slot], in_all.at[slot], pair_send, pair_recv, dp, partner
        )

    def c_out(slot, steps):
        for step in steps:
            c_copy(slot, step).start()

    def arrive(step):
        slot = at_z(step)
        c_copy(slot, 1).wait_recv()
        return slot

    pl.semaphore_wait(known.at[len(VOUCH) - 1], 2)
    c_out(mp, FAR + NEAR)
    pair_copy(mp).start()
    d_own(False)

    def d_onward(steps):
        for step in steps:
            for half in (0, 1):
                slot = at_x(step) if half == 0 else at_y(step)
                d_copy(half, slot, NX - step, True).wait_recv()
                for onward in (2, 1, 3):
                    d_copy(half, slot, onward, False).start()

    def c_onward(step):
        slot = arrive(step)
        part = in_all.at[slot, pl.ds(CT, QT) if step > 0 else pl.ds(0, CT)]
        away = at_z(-LAST if step > 0 else LAST)
        copy(part, part, c_send, c_recv.at[slot], dp, away).start()
        for onward in ONWARD:
            c_out(slot, (-onward if step > 0 else onward,))

    def c_pair(steps):
        for step in steps:
            pair_copy(arrive(step)).start()

    d_onward((1, 3, 2))
    c_onward(FAR[0])
    c_onward(FAR[1])
    for step in FAR:
        pair_copy(at_z(step)).start()
    c_pair(NEAR + REST)

    rest = out_all.at[pl.ds(0, 12)]
    pltpu.make_async_copy(rest, rest, d_rest).wait()
    half_line = in_all.at[pl.ds(0, NZ)]
    pltpu.make_async_copy(half_line, half_line, pair_recv).wait()

    tokens = QUERIES * QLEN
    in_q = in_all[:, pl.ds(CT, QT), :].reshape(tokens, WI)
    folded = []
    for cand in range(CANDS):
        in_cand = in_all[pl.ds(cand * 16, 16), pl.ds(0, CT), :].reshape(CLEN, WI)
        out_cand = out_all[pl.ds(cand * 8, 8), pl.ds(0, CO), :].reshape(CLEN, WO)
        grad = lax.dot_general(
            in_cand, out_cand, (((0,), (0,)), ((), ())), preferred_element_type=jnp.float32
        )
        weight = (grad * recip[...]).astype(jnp.bfloat16)
        applied = jnp.dot(in_q, weight, preferred_element_type=jnp.float32)
        out_query = out_all[:, pl.ds(CO, QO), :].reshape(tokens, WO)
        product = applied * out_query.astype(jnp.float32)
        narrow = product[:, 0:128]
        for part in range(1, WO // 128):
            narrow += product[:, part * 128 : part * 128 + 128]
        narrow = narrow * maskcol[...]
        folded.append(jnp.sum(narrow.reshape(QUERIES, QLEN, 128), axis=1))
    column = jnp.sum(jnp.concatenate(folded, axis=0), axis=1, keepdims=True)
    count = QUERIES * CANDS
    rows = lax.broadcasted_iota(jnp.int32, (count, 128), 0)
    lanes = lax.broadcasted_iota(jnp.int32, (count, 128), 1)
    line = jnp.sum(
        jnp.where(rows == lanes, jnp.broadcast_to(column, (count, 128)), 0.0), axis=0, keepdims=True
    )

    flat = dp * 2 + core
    part1[flat] = line
    plane = [(up, over, other) for up in range(NX) for over in range(NX) for other in range(2)]
    plane.sort(key=lambda o: (-min(o[0], NX - o[0]) - min(o[1], NX - o[1]), -o[2]))
    plane.remove((0, 0, 0))
    e_copies = []
    for index, (up, over, other) in enumerate(plane):
        e_copies.append(copy(
            part1.at[flat], part1.at[flat], e_send, e_recv,
            in_plane(up, over), partner if other else mp,
        ))
    for each in e_copies:
        each.start()
    others = part1.at[pl.ds(0, len(e_copies))]
    pltpu.make_async_copy(others, others, e_recv).wait()
    part2[z] = jnp.sum(part1[...], axis=0)

    f_copies = []
    for step in (8, 7, -7, 6, -6, 5, -5, 4, -4, 3, -3, 2, -2, 1, -1):
        f_copies.append(copy(
            part2.at[z], part2.at[z], f_send, f_recv, dp, at_z(step)
        ))
    for each in f_copies:
        each.start()
    for each in sends:
        each.wait_send()
    pltpu.make_async_copy(others, others, e_send).wait()
    gone = in_all.at[pl.ds(0, NZ - 1)]
    pltpu.make_async_copy(gone, gone, c_send).wait()
    gone = out_all.at[pl.ds(0, 15)]
    pltpu.make_async_copy(gone, gone, d_send).wait()

    pltpu.make_async_copy(half_line, half_line, pair_send).wait()
    others = part2.at[pl.ds(0, len(f_copies))]
    pltpu.make_async_copy(others, others, f_send).wait()
    pltpu.make_async_copy(others, others, f_recv).wait()
    total = jnp.sum(part2[...], axis=0) * SCALE
    for cand in range(CANDS):
        scores[pl.ds(cand, 1), :] = total[:, cand * QUERIES : cand * QUERIES + QUERIES]


def local(*args):
    dma = pltpu.SemaphoreType.DMA
    by_cand = pl.pallas_call(
        kernel,
        name="scores",
        out_shape=pltpu.VMEM((CANDS, QUERIES), jnp.float32),
        in_specs=[pl.BlockSpec(memory_space=pl.ANY)] * 8,
        out_specs=pl.BlockSpec(memory_space=pltpu.VMEM),
        scratch_shapes=[
            pltpu.VMEM((NX, CT + QT, WI), jnp.bfloat16),
            pltpu.VMEM((2, CO + QO, WO), jnp.bfloat16),
            pltpu.VMEM((NX * WI, WI), jnp.bfloat16),
            pltpu.VMEM((2 * WO, WO), jnp.bfloat16),
            pltpu.VMEM((WI, WO), jnp.float32),
            pltpu.VMEM((QUERIES, QLEN), jnp.int32),
            pltpu.VMEM((QUERIES * QLEN, 128), jnp.float32),
            pltpu.VMEM((WI, WO), jnp.float32),
            pltpu.VMEM((2 * NZ, CT + QT, WI), jnp.bfloat16),
            pltpu.VMEM((NX * NX, CO + QO, WO), jnp.bfloat16),
            pltpu.VMEM((32, 1, 128), jnp.float32),
            pltpu.VMEM((NZ, 1, 128), jnp.float32),
            dma((8,)),
            dma((NX, 2)),
            dma((NX, 2)),
            dma((2,)),
            dma((2,)),
            dma,
            dma((2 * NZ,)),
            dma,
            dma,
            dma((2, NX)),
            dma,
            dma,
            dma,
            dma,
            dma,
            dma,
            pltpu.SemaphoreType.REGULAR((3,)),
        ],
        compiler_params=pltpu.CompilerParams(
            collective_id=0, has_side_effects=True, vmem_limit_bytes=60 << 20
        ),
    )(*args)
    return by_cand.T


def solution(mesh):
    return jax.shard_map(
        local,
        mesh=mesh,
        in_specs=(
            P("mp", "dp"),
            P("dp", "mp"),
            P("mp", "dp"),
            P("dp", "mp"),
            P(),
            P(None, "dp"),
            P(None, "mp"),
            P("dp", "mp"),
        ),
        out_specs=P(),
        check_vma=False,
    )
```

```python
import functools
import math

import jax
import jax.numpy as jnp
from jax import lax
from jax.experimental import pallas as pl
from jax.experimental.pallas import tpu as pltpu
from jax.sharding import PartitionSpec as P

DW = 4096
FW = 16384
QUERIES = 16
QLEN = 32
CLEN = 512
CANDS = 2
DAMPING = 0.1
FAR, NEAR = (4, -4), (3, -3, 2, -2, 1, -1)
ONWARD = (3, 2, 1)
LAST = 4
GREET = (2, -2, 1, -1)
VOUCH = (2,)
REST = (5, -5, 6, -6, 7, -7, 8)
SCALE = 1.0 / math.sqrt(QLEN * CLEN * DW * FW)

NX = 4
NZ = 16
CT, QT = 32, 16
CO, QO = 64, 32
WI, WO = 256, 512
HALF = (CO + QO) // 2

MESH = pl.DeviceIdType.MESH


def kernel(
    act_c, out_c, act_q, out_q, mask, in_basis, out_basis, eig,
    scores,
    actw, outw, basis_i, basis_o, eigv, maskv, maskcol, recip, in_all, out_all, part1, part2,
    load_sem, a_send, a_recv, b_send, b_recv, c_send, c_recv, pair_send, d_send, d_recv,
    e_send, e_recv, f_send, f_recv, pair_recv, d_rest, known,
):
    dp = lax.axis_index("dp")
    mp = lax.axis_index("mp")
    y, x = lax.div(dp, NX), lax.rem(dp, NX)
    z, core = lax.div(mp, 2), lax.rem(mp, 2)
    partner = mp + 1 - 2 * core

    def at_z(step):
        return lax.rem(z + step + NZ, NZ) * 2 + core

    @functools.cache
    def in_plane(up, over):
        return lax.rem(y + up, NX) * NX + lax.rem(x + over, NX)

    def at_x(step):
        return in_plane(0, step)

    def at_y(step):
        return in_plane(step, 0)

    def copy(src, dst, send, recv, to_dp, to_mp):
        return pltpu.make_async_remote_copy(
            src_ref=src, dst_ref=dst, send_sem=send, recv_sem=recv,
            device_id=(to_dp, to_mp), device_id_type=MESH,
        )

    loads = [
        pltpu.make_async_copy(act_c, actw.at[x, pl.ds(0, CT)], load_sem.at[0]),
        pltpu.make_async_copy(act_q, actw.at[x, pl.ds(CT, QT)], load_sem.at[1]),
        pltpu.make_async_copy(out_c, outw.at[core, pl.ds(0, CO)], load_sem.at[2]),
        pltpu.make_async_copy(out_q, outw.at[core, pl.ds(CO, QO)], load_sem.at[3]),
        pltpu.make_async_copy(out_basis, basis_o, load_sem.at[4]),
        pltpu.make_async_copy(in_basis, basis_i, load_sem.at[5]),
        pltpu.make_async_copy(mask, maskv, load_sem.at[6]),
        pltpu.make_async_copy(eig, eigv, load_sem.at[7]),
    ]

    barrier = pltpu.get_barrier_semaphore()
    greet = [(dp, at_z(step)) for step in GREET]
    greet += [(at_x(step), mp) for step in (2, 1, 3)]
    greet += [(at_y(step), mp) for step in (2, 1, 3)]
    greet += [(dp, partner)]
    for peer in greet:
        pl.semaphore_signal(barrier, inc=1, device_id=peer, device_id_type=MESH)
    for load in loads[2:5]:
        load.start()
    pl.semaphore_wait(barrier, len(greet))

    def vouch(level, reach):
        for step in (reach, -reach):
            pl.semaphore_signal(
                known.at[level], inc=1, device_id=(dp, at_z(step)), device_id_type=MESH
            )

    vouch(0, VOUCH[0])

    sends = []
    a_copies = []
    for step in (2, 1, 3):
        for part, (src, first, count) in enumerate(((act_c, 0, CT), (act_q, CT, QT))):
            a_copies.append(copy(
                src, actw.at[x, pl.ds(first, count)], a_send.at[step, part], a_recv.at[step, part],
                at_x(step), mp,
            ))
    b_copies = []
    for part, (src, first, count) in enumerate(((out_c, 0, CO), (out_q, CO, QO))):
        b_copies.append(copy(
            src, outw.at[core, pl.ds(first, count)], b_send.at[part], b_recv.at[part], dp, partner
        ))
    sends += a_copies + b_copies
    for each in sends:
        each.start()
    for load in loads[:2] + loads[5:]:
        load.start()

    for load in loads[2:5]:
        load.wait()
    for each in b_copies:
        each.wait_recv()
    turned = jnp.dot(outw[0], basis_o[pl.ds(0, WO), :], preferred_element_type=jnp.float32)
    turned += jnp.dot(outw[1], basis_o[pl.ds(WO, WO), :], preferred_element_type=jnp.float32)
    out_all[dp] = turned.astype(jnp.bfloat16)

    def d_copy(half, slot, step, first):
        to_dp = at_x(step) if (half == 0) == first else at_y(step)
        part = out_all.at[slot, pl.ds(half * HALF, HALF)]
        return copy(part, part, d_send, d_recv.at[half, step] if first else d_rest, to_dp, mp)

    def d_own(first):
        for step in (2, 1, 3):
            for half in (0, 1):
                d_copy(half, dp, step, first).start()

    d_own(True)
    for level, reach in enumerate(VOUCH[1:]):
        pl.semaphore_wait(known.at[level], 2)
        vouch(level + 1, reach)

    loads[6].wait()
    rows = lax.broadcasted_iota(jnp.int32, (QLEN, QLEN), 0)
    lanes = lax.broadcasted_iota(jnp.int32, (QLEN, QLEN), 1)
    for q in range(QUERIES):
        spread = jnp.broadcast_to(maskv[pl.ds(q, 1), :].astype(jnp.float32), (QLEN, QLEN))
        column = jnp.sum(jnp.where(rows == lanes, spread, 0.0), axis=1, keepdims=True)
        maskcol[pl.ds(q * QLEN, QLEN), :] = jnp.broadcast_to(column, (QLEN, 128))
    loads[7].wait()
    recip[...] = 1.0 / (eigv[...] + DAMPING)

    for load in (loads[0], loads[1], loads[5]):
        load.wait()
    for each in a_copies:
        each.wait_recv()
    turned = jnp.dot(actw[0], basis_i[pl.ds(0, WI), :], preferred_element_type=jnp.float32)
    for piece in range(1, NX):
        turned += jnp.dot(
            actw[piece], basis_i[pl.ds(piece * WI, WI), :], preferred_element_type=jnp.float32
        )
    in_all[mp] = turned.astype(jnp.bfloat16)

    def c_copy(slot, step):
        return copy(
            in_all.at[slot], in_all.at[slot], c_send, c_recv.at[slot], dp, at_z(step)
        )

    def pair_copy(slot):
        return copy(
            in_all.at[slot], in_all.at[slot], pair_send, pair_recv, dp, partner
        )

    def c_out(slot, steps):
        for step in steps:
            c_copy(slot, step).start()

    def arrive(step):
        slot = at_z(step)
        c_copy(slot, 1).wait_recv()
        return slot

    pl.semaphore_wait(known.at[len(VOUCH) - 1], 2)
    c_out(mp, FAR + NEAR)
    pair_copy(mp).start()
    d_own(False)

    def d_onward(steps):
        for step in steps:
            for half in (0, 1):
                slot = at_x(step) if half == 0 else at_y(step)
                d_copy(half, slot, NX - step, True).wait_recv()
                for onward in (2, 1, 3):
                    d_copy(half, slot, onward, False).start()

    def c_onward(step):
        slot = arrive(step)
        part = in_all.at[slot, pl.ds(CT, QT) if step > 0 else pl.ds(0, CT)]
        away = at_z(-LAST if step > 0 else LAST)
        copy(part, part, c_send, c_recv.at[slot], dp, away).start()
        for onward in ONWARD:
            c_out(slot, (-onward if step > 0 else onward,))

    def c_pair(steps):
        for step in steps:
            pair_copy(arrive(step)).start()

    d_onward((1, 3, 2))
    c_onward(FAR[0])
    c_onward(FAR[1])
    for step in FAR:
        pair_copy(at_z(step)).start()
    c_pair(NEAR + REST)

    rest = out_all.at[pl.ds(0, 12)]
    pltpu.make_async_copy(rest, rest, d_rest).wait()
    half_line = in_all.at[pl.ds(0, NZ)]
    pltpu.make_async_copy(half_line, half_line, pair_recv).wait()

    tokens = QUERIES * QLEN
    in_q = in_all[:, pl.ds(CT, QT), :].reshape(tokens, WI)
    folded = []
    for cand in range(CANDS):
        in_cand = in_all[pl.ds(cand * 16, 16), pl.ds(0, CT), :].reshape(CLEN, WI)
        out_cand = out_all[pl.ds(cand * 8, 8), pl.ds(0, CO), :].reshape(CLEN, WO)
        grad = lax.dot_general(
            in_cand, out_cand, (((0,), (0,)), ((), ())), preferred_element_type=jnp.float32
        )
        weight = (grad * recip[...]).astype(jnp.bfloat16)
        applied = jnp.dot(in_q, weight, preferred_element_type=jnp.float32)
        out_query = out_all[:, pl.ds(CO, QO), :].reshape(tokens, WO)
        product = applied * out_query.astype(jnp.float32)
        narrow = product[:, 0:128]
        for part in range(1, WO // 128):
            narrow += product[:, part * 128 : part * 128 + 128]
        narrow = narrow * maskcol[...]
        folded.append(jnp.sum(narrow.reshape(QUERIES, QLEN, 128), axis=1))
    column = jnp.sum(jnp.concatenate(folded, axis=0), axis=1, keepdims=True)
    count = QUERIES * CANDS
    rows = lax.broadcasted_iota(jnp.int32, (count, 128), 0)
    lanes = lax.broadcasted_iota(jnp.int32, (count, 128), 1)
    line = jnp.sum(
        jnp.where(rows == lanes, jnp.broadcast_to(column, (count, 128)), 0.0), axis=0, keepdims=True
    )

    flat = dp * 2 + core
    part1[flat] = line
    plane = [(up, over, other) for up in range(NX) for over in range(NX) for other in range(2)]
    plane.sort(key=lambda o: (-min(o[0], NX - o[0]) - min(o[1], NX - o[1]), -o[2]))
    plane.remove((0, 0, 0))
    e_copies = []
    for index, (up, over, other) in enumerate(plane):
        e_copies.append(copy(
            part1.at[flat], part1.at[flat], e_send, e_recv,
            in_plane(up, over), partner if other else mp,
        ))
    for each in e_copies:
        each.start()
    others = part1.at[pl.ds(0, len(e_copies))]
    pltpu.make_async_copy(others, others, e_recv).wait()
    part2[z] = jnp.sum(part1[...], axis=0)

    f_copies = []
    for step in (8, 7, -7, 6, -6, 5, -5, 4, -4, 3, -3, 2, -2, 1, -1):
        f_copies.append(copy(
            part2.at[z], part2.at[z], f_send, f_recv, dp, at_z(step)
        ))
    for each in f_copies:
        each.start()
    for each in sends:
        each.wait_send()
    pltpu.make_async_copy(others, others, e_send).wait()
    gone = in_all.at[pl.ds(0, NZ - 1)]
    pltpu.make_async_copy(gone, gone, c_send).wait()
    gone = out_all.at[pl.ds(0, 15)]
    pltpu.make_async_copy(gone, gone, d_send).wait()

    pltpu.make_async_copy(half_line, half_line, pair_send).wait()
    others = part2.at[pl.ds(0, len(f_copies))]
    pltpu.make_async_copy(others, others, f_send).wait()
    pltpu.make_async_copy(others, others, f_recv).wait()
    total = jnp.sum(part2[...], axis=0) * SCALE
    for cand in range(CANDS):
        scores[pl.ds(cand, 1), :] = total[:, cand * QUERIES : cand * QUERIES + QUERIES]


def local(*args):
    dma = pltpu.SemaphoreType.DMA
    by_cand = pl.pallas_call(
        kernel,
        name="scores",
        out_shape=pltpu.VMEM((CANDS, QUERIES), jnp.float32),
        in_specs=[pl.BlockSpec(memory_space=pl.ANY)] * 8,
        out_specs=pl.BlockSpec(memory_space=pltpu.VMEM),
        scratch_shapes=[
            pltpu.VMEM((NX, CT + QT, WI), jnp.bfloat16),
            pltpu.VMEM((2, CO + QO, WO), jnp.bfloat16),
            pltpu.VMEM((NX * WI, WI), jnp.bfloat16),
            pltpu.VMEM((2 * WO, WO), jnp.bfloat16),
            pltpu.VMEM((WI, WO), jnp.float32),
            pltpu.VMEM((QUERIES, QLEN), jnp.int32),
            pltpu.VMEM((QUERIES * QLEN, 128), jnp.float32),
            pltpu.VMEM((WI, WO), jnp.float32),
            pltpu.VMEM((2 * NZ, CT + QT, WI), jnp.bfloat16),
            pltpu.VMEM((NX * NX, CO + QO, WO), jnp.bfloat16),
            pltpu.VMEM((32, 1, 128), jnp.float32),
            pltpu.VMEM((NZ, 1, 128), jnp.float32),
            dma((8,)),
            dma((NX, 2)),
            dma((NX, 2)),
            dma((2,)),
            dma((2,)),
            dma,
            dma((2 * NZ,)),
            dma,
            dma,
            dma((2, NX)),
            dma,
            dma,
            dma,
            dma,
            dma,
            dma,
            pltpu.SemaphoreType.REGULAR((3,)),
        ],
        compiler_params=pltpu.CompilerParams(
            collective_id=0, has_side_effects=True, vmem_limit_bytes=60 << 20
        ),
    )(*args)
    return by_cand.T


def solution(mesh):
    return jax.shard_map(
        local,
        mesh=mesh,
        in_specs=(
            P("mp", "dp"),
            P("dp", "mp"),
            P("mp", "dp"),
            P("dp", "mp"),
            P(),
            P(None, "dp"),
            P(None, "mp"),
            P("dp", "mp"),
        ),
        out_specs=P(),
        check_vma=False,
    )
```
